32 devices in a mesh: tm: 8 (over y, x, core), tile: 4 (over z).
Axes of the slice: x: 2, y: 2, z: 4, core: 2. Of those that a mesh axis runs over, the one named last changes fastest.
Arguments:
- velocity_u: float32 [384, 2, 16, 1024], P('tm', None, None, 'tile'), may hold values from -12 to 12
- velocity_v: float32 [384, 2, 16, 1024], P('tm', None, None, 'tile'), may hold values from -12 to 12
- land_sea: int32 [16, 1024], P(None, 'tile'), may hold values 0 or 1
- bottom_level: int32 [16, 1024], P(None, 'tile'), may hold values from 0 to 2
- spacing_x: float32 [16, 1024], P(None, 'tile'), may hold values from 0.5 to 2
- spacing_y: float32 [16, 1024], P(None, 'tile'), may hold values from 0.5 to 2
Outputs:
- conversion_maps: bfloat16 [384, 2, 16, 1024], P('tm', None, None, 'tile')
- mean_map: float32 [2, 16, 1024], P(None, None, 'tile')
The draws below stay inside these ranges and needn't reach their ends.
All inputs are finite; a program needn't handle non-finite values. No bound on the sum of `land_sea` on one device may be relied on, other than what follows from the above.
Results may differ from the reference program's by a relative error of at most 0.001.
Values sent between devices are 32-bit elements; how exact they have to be, the bound alone decides.
A program may use at most 64 MiB of HBM per device.

```python
import math
import jax
import jax.numpy as jnp
from jax import lax

HALF = 24
SNAPS = 48
LEVELS = 2
ROWS = 16
TOTAL = 384
NX = 1024


def noisy_series(key, series_tag):
    series_key = jax.random.fold_in(key, series_tag)
    full_shape = (TOTAL + 1, LEVELS, ROWS, NX)
    noise_field = jnp.clip(jax.random.normal(series_key, full_shape, jnp.float32), -4.0, 4.0)
    return 1.5 * (noise_field[1:] - noise_field[:-1])


def draw_velocity_u(key, part):
    return noisy_series(key, 101)


def draw_velocity_v(key, part):
    return noisy_series(key, 202)


def place_ends(array, stream_key, smallest, top_value):
    shape = array.shape
    place = [jax.random.randint(jax.random.fold_in(stream_key, axis), (), 0, shape[axis]) for axis in range(len(shape))]
    array = array.at[tuple(place)].set(smallest)
    longest = shape.index(max(shape))
    place[longest] = (place[longest] + 1) % shape[longest]
    return array.at[tuple(place)].set(top_value)


def level_of(stream_key, dims, shards, low, high):
    gain = 1.0
    for dim, shards_of in shards:
        draws = jax.random.uniform(jax.random.fold_in(jax.random.fold_in(stream_key, 6), dim), (shards_of,), jnp.float32, low / len(shards), high / len(shards))
        gain = gain * jnp.repeat(jnp.exp(draws), dims[dim] // shards_of).reshape((-1,) + (1,) * (len(dims) - 1 - dim))
    return gain


def setup_inputs(seed: int = 0) -> dict:
    keys = jax.random.split(jax.random.key(seed), 7)
    velocity_u = draw_velocity_u(jax.random.fold_in(keys[6], 71), 0)
    velocity_v = draw_velocity_v(jax.random.fold_in(keys[6], 71), 0)
    land_sea = place_ends((jax.random.randint(keys[2], (ROWS, NX), 0, 10) < 9).astype(jnp.int32), jax.random.fold_in(keys[2], 1), 0, 1)
    bottom_level = place_ends(jax.random.randint(keys[3], (ROWS, NX), 0, LEVELS + 1), jax.random.fold_in(keys[3], 1), 0, LEVELS).astype(jnp.int32)
    spacing_x = jnp.clip(jnp.exp(math.log(2.0) - 1.3862944 * jax.random.uniform(keys[4], (ROWS, NX), jnp.float32) ** level_of(keys[4], (ROWS, NX), ((1, 4),), -0.2, 0.2)), 0.5, 2.0)
    spacing_y = jnp.clip(jnp.exp(math.log(2.0) - 1.3862944 * jax.random.uniform(keys[5], (ROWS, NX), jnp.float32) ** level_of(keys[5], (ROWS, NX), ((1, 4),), -0.2, 0.2)), 0.5, 2.0)
    return dict(velocity_u=velocity_u, velocity_v=velocity_v, land_sea=land_sea, bottom_level=bottom_level, spacing_x=spacing_x, spacing_y=spacing_y)


cutoff_freq = 1.0 / 40.0


def band_matrix(count):
    out_rows = jnp.arange(count, dtype=jnp.int32)[:, None]
    in_cols = jnp.arange(count + 2 * HALF, dtype=jnp.int32)[None, :]
    offset = (in_cols - out_rows - HALF).astype(jnp.float32)
    weights = 2.0 * cutoff_freq * jnp.sinc(2.0 * cutoff_freq * offset) * jnp.sinc(offset / HALF)
    return jnp.where(jnp.abs(offset) <= HALF, weights, jnp.zeros_like(weights))


def lowpass(padded, validity, blocks, block):
    matrix = band_matrix(block)

    def one_block(block_id):
        start = (block_id * block).astype(jnp.int32)
        window = lax.dynamic_slice_in_dim(padded, start, block + 2 * HALF, 0)
        valid_part = lax.dynamic_slice_in_dim(validity, start, block + 2 * HALF, 0)
        weighted = jnp.dot(matrix, window, precision=lax.Precision.HIGHEST, preferred_element_type=jnp.float32)
        weight_sum = jnp.dot(matrix, valid_part, precision=lax.Precision.HIGHEST, preferred_element_type=jnp.float32)
        return weighted / weight_sum[:, None]

    result = lax.map(one_block, jnp.arange(blocks, dtype=jnp.int32))
    return result.reshape(blocks * block, padded.shape[1])


def wet_cells(land_sea, bottom_level, levels):
    level_ids = jnp.arange(levels, dtype=jnp.int32)[:, None, None]
    return ((land_sea[None] == 1) & (level_ids < bottom_level[None])).astype(jnp.float32)


def conversion_terms(extended, eddies, wet_mask, spacing_x, spacing_y):
    grad_x = (extended[..., 2:] - extended[..., :-2]) * (0.5 / spacing_x)
    centre = extended[..., 1:-1]
    row_padded = jnp.pad(centre, ((0, 0), (0, 0), (0, 0), (1, 1), (0, 0)))
    grad_y = (row_padded[..., 2:, :] - row_padded[..., :-2, :]) * (0.5 / spacing_y)
    eddy_u = eddies[:, 0]
    eddy_v = eddies[:, 1]
    total = eddy_u * eddy_u * grad_x[:, 0] + eddy_u * eddy_v * (grad_y[:, 0] + grad_x[:, 1]) + eddy_v * eddy_v * grad_y[:, 1]
    return -wet_mask[None] * total


def reference(velocity_u, velocity_v, land_sea, bottom_level, spacing_x, spacing_y):
    length = velocity_u.shape[0]
    stacked = jnp.stack([velocity_u, velocity_v], axis=1)
    flattened = stacked.reshape(length, -1)
    padded = jnp.pad(flattened, ((HALF, HALF), (0, 0)))
    validity = jnp.pad(jnp.ones((length,), jnp.float32), (HALF, HALF))
    mean_flow = lowpass(padded, validity, length // SNAPS, SNAPS).reshape(stacked.shape)
    eddies = stacked - mean_flow
    wet_mask = wet_cells(land_sea, bottom_level, stacked.shape[2])
    masked = mean_flow * wet_mask[None, None]
    extended = jnp.pad(masked, ((0, 0), (0, 0), (0, 0), (0, 0), (1, 1)))
    conversion = conversion_terms(extended, eddies, wet_mask, spacing_x, spacing_y)
    return conversion.astype(jnp.bfloat16), jnp.sum(conversion, axis=0) / length
```

```python
import functools

import jax
import jax.numpy as jnp
import numpy as np
from jax import lax
from jax.experimental import pallas as pl
from jax.experimental.pallas import tpu as pltpu
from jax.sharding import PartitionSpec as P

HALF = 24
CUTOFF = 1.0 / 40.0
LANES = 128
CHUNK = 8
MESH = pl.DeviceIdType.MESH


def band_parts(count):
    offset = (np.arange(count + 2 * HALF)[None, :] - np.arange(count)[:, None] - HALF).astype(np.float64)
    weights = 2.0 * CUTOFF * np.sinc(2.0 * CUTOFF * offset) * np.sinc(offset / HALF)
    weights = np.where(np.abs(offset) <= HALF, weights, 0.0).astype(np.float32)
    own = weights[:, HALF : HALF + count]
    halo = np.concatenate([weights[:, :HALF], weights[:, HALF + count :]], axis=1)
    return own, halo


def dot(a, b):
    return jnp.dot(a, b, precision=lax.Precision.HIGHEST, preferred_element_type=jnp.float32)


def kernel(
    n_tm, n_tile, levels,
    u_ref, v_ref, land_ref, bottom_ref, sx_ref, sy_ref, own_ref, halo_w_ref,
    conv_ref, mean_ref,
    x, halo, mm, cf, wet, cx, cy, sums, part, edge, edge_halo, edge_mean, edge_in,
    x_sem, bulk_send, bulk_recv, edge_send, edge_recv, em_send, em_recv, part_send, part_recv,
):
    snaps, cells, width = u_ref.shape
    rows = cells // levels
    t = lax.axis_index("tm")
    z = lax.axis_index("tile")
    chunks = cells // CHUNK
    fields = (u_ref, v_ref)

    barrier = pltpu.get_barrier_semaphore()
    for k in range(1, n_tm):
        pl.semaphore_signal(barrier, inc=1, device_id={"tm": lax.rem(t + k, n_tm)}, device_id_type=MESH)

    @pl.when(z > 0)
    def _():
        pl.semaphore_signal(barrier, inc=1, device_id={"tile": z - 1}, device_id_type=MESH)

    @pl.when(z < n_tile - 1)
    def _():
        pl.semaphore_signal(barrier, inc=1, device_id={"tile": z + 1}, device_id_type=MESH)

    def local(f, h):
        return pltpu.make_async_copy(
            fields[f].at[:, :, pl.ds(h * LANES, LANES)], x.at[f, h], x_sem.at[f, h]
        )

    for f in range(2):
        for h in range(2):
            local(f, h).start()

    pl.semaphore_wait(barrier, n_tm - 1 + (z > 0).astype(jnp.int32) + (z < n_tile - 1).astype(jnp.int32))

    def bulk(side, c, f, h):
        first = snaps - HALF if side == 0 else 0
        to = t + 1 if side == 0 else t - 1
        return pltpu.make_async_remote_copy(
            src_ref=fields[f].at[pl.ds(first, HALF), pl.ds(c * CHUNK, CHUNK), pl.ds(h * LANES, LANES)],
            dst_ref=halo.at[side, f, h, :, pl.ds(c * CHUNK, CHUNK), :],
            send_sem=bulk_send.at[side, c, f, h],
            recv_sem=bulk_recv.at[side, c, f, h],
            device_id={"tm": to},
            device_id_type=MESH,
        )

    def edge_copy(side):
        first = snaps - HALF if side == 0 else 0
        to = t + 1 if side == 0 else t - 1
        return pltpu.make_async_remote_copy(
            src_ref=edge.at[pl.ds(first, HALF), :],
            dst_ref=edge_halo.at[side],
            send_sem=edge_send.at[side],
            recv_sem=edge_recv.at[side],
            device_id={"tm": to},
            device_id_type=MESH,
        )

    def mean_copy(side):
        to = z + 1 if side == 0 else z - 1
        return pltpu.make_async_remote_copy(
            src_ref=edge_mean,
            dst_ref=edge_in.at[side],
            send_sem=em_send.at[side],
            recv_sem=em_recv.at[side],
            device_id={"tile": to},
            device_id_type=MESH,
        )

    def part_copy(l, k, slot):
        return pltpu.make_async_remote_copy(
            src_ref=part.at[slot, l],
            dst_ref=part.at[slot, l],
            send_sem=part_send.at[l, k],
            recv_sem=part_recv.at[l, k],
            device_id={"tm": lax.rem(t + k, n_tm)},
            device_id_type=MESH,
        )

    sends = (t < n_tm - 1, t > 0)
    receives = (t > 0, t < n_tm - 1)
    z_sends = (z < n_tile - 1, z > 0)
    z_receives = (z > 0, z < n_tile - 1)

    for c in range(chunks):
        for side in range(2):

            @pl.when(sends[side])
            def _():
                for f in range(2):
                    for h in range(2):
                        bulk(side, c, f, h).start()

    for side in range(2):

        @pl.when(jnp.logical_not(receives[side]))
        def _():
            halo[side] = jnp.zeros(halo.shape[1:], jnp.float32)
            edge_halo[side] = jnp.zeros(edge_halo.shape[1:], jnp.float32)

        @pl.when(jnp.logical_not(z_receives[side]))
        def _():
            edge_in[side] = jnp.zeros(edge_in.shape[1:], jnp.float32)

    for l in range(levels):
        is_wet = (land_ref[...] == 1) & (l < bottom_ref[...])
        level_wet = jnp.where(is_wet, 1.0, 0.0).astype(jnp.float32)
        for j in range(rows):
            wet[l * rows + j] = level_wet[j : j + 1, :]
    all_x, all_y = 0.5 / sx_ref[...], 0.5 / sy_ref[...]
    for j in range(rows):
        cx[j] = all_x[j : j + 1, :]
        cy[j] = all_y[j : j + 1, :]
    for f in range(2):
        for l in range(levels):
            for j in (0, rows + 1):
                mm[f, l, j] = jnp.zeros((snaps, width), jnp.float32)
    column = lax.broadcasted_iota(jnp.int32, (snaps, 2 * HALF), 1)
    valid = ((column >= HALF) | (t > 0)) & ((column < HALF) | (t < n_tm - 1))
    own_w = own_ref[...]
    halo_w = jnp.where(valid, halo_w_ref[...], 0.0)
    weight_sum = jnp.sum(own_w, axis=1, keepdims=True) + jnp.sum(halo_w, axis=1, keepdims=True)
    own_w = own_w / weight_sum
    halo_w = halo_w / weight_sum

    for f in range(2):
        for h in range(2):
            local(f, h).wait()

    def series(ref, count, r):
        return ref.reshape(count * cells, LANES)[pl.ds(r, count, stride=cells), :]

    lane = lax.broadcasted_iota(jnp.int32, (snaps, LANES), 1)

    def pack(r, acc):
        for f in range(2):
            q = f * cells + r
            first = series(x.at[f, 0], snaps, r) * wet[r][:, :LANES]
            acc = jnp.where(lane == q, pltpu.roll(first, q, 1), acc)
            q = (2 + f) * cells + r
            last = series(x.at[f, 1], snaps, r) * wet[r][:, width - LANES :]
            acc = jnp.where(lane == q, pltpu.roll(last, lax.rem(q + 1, LANES), 1), acc)
        return acc

    edge[...] = lax.fori_loop(0, cells, pack, jnp.zeros((snaps, LANES), jnp.float32))
    for side in range(2):

        @pl.when(sends[side])
        def _():
            edge_copy(side).start()

    def own_part(r, carry):
        l, j = r // rows, lax.rem(r, rows)
        for f in range(2):
            block = jnp.concatenate([series(x.at[f, h], snaps, r) for h in range(2)], axis=1)
            mm[f, l, j + 1] = dot(own_w, block)
        return carry

    lax.fori_loop(0, cells, own_part, 0)

    for side in range(2):

        @pl.when(receives[side])
        def _():
            edge_copy(side).wait_recv()

    edge_mean[...] = dot(own_w, edge[...]) + dot(
        halo_w, jnp.concatenate([edge_halo[0], edge_halo[1]], axis=0)
    )
    for side in range(2):

        @pl.when(z_sends[side])
        def _():
            mean_copy(side).start()

    wide = lax.broadcasted_iota(jnp.int32, (snaps, width), 1)

    def halo_part(r, carry):
        l, j = r // rows, lax.rem(r, rows)
        mask = wet[r]
        for f in range(2):
            block = jnp.concatenate(
                [
                    jnp.concatenate([series(halo.at[s, f, h], HALF, r) for h in range(2)], axis=1)
                    for s in range(2)
                ],
                axis=0,
            )
            mm[f, l, j + 1] = (mm[f, l, j + 1] + dot(halo_w, block)) * mask
        return carry

    def grad_x(f, r, masked, scale):
        q = (2 + f) * cells + r
        before = pltpu.roll(edge_in[0], lax.rem(2 * LANES - q, LANES), 1)
        q = f * cells + r
        after = pltpu.roll(edge_in[1], lax.rem(2 * LANES - 1 - q, LANES), 1)
        before = jnp.concatenate([before, before], axis=1)
        after = jnp.concatenate([after, after], axis=1)
        behind = jnp.where(wide == 0, before, pltpu.roll(masked, 1, 1))
        ahead = jnp.where(wide == width - 1, after, pltpu.roll(masked, width - 1, 1))
        return (ahead - behind) * scale

    def convert(l):
        def body(j, carry):
            r = l * rows + j
            mask = wet[r]
            scale_x = cx[j]
            scale_y = cy[j]
            eddy, gx, gy = [], [], []
            for f in range(2):
                masked = mm[f, l, j + 1]
                raw = jnp.concatenate([series(x.at[f, h], snaps, r) for h in range(2)], axis=1)
                eddy.append(raw - masked)
                gx.append(grad_x(f, r, masked, scale_x))
                gy.append((mm[f, l, j + 2] - mm[f, l, j]) * scale_y)
            eu, ev = eddy
            total = eu * eu * gx[0] + eu * ev * (gy[0] + gx[1]) + ev * ev * gy[1]
            conversion = -mask * total
            for h in range(2):
                cf.at[h].reshape(snaps * cells, LANES)[pl.ds(r, snaps, stride=cells), :] = conversion[
                    :, h * LANES : (h + 1) * LANES
                ]
            sums[r] = jnp.sum(conversion, axis=0, keepdims=True)
            return carry

        return body

    per_level = rows // CHUNK
    for c in range(chunks):
        for side in range(2):

            @pl.when(receives[side])
            def _():
                for f in range(2):
                    for h in range(2):
                        bulk(side, c, f, h).wait_recv()

        lax.fori_loop(c * CHUNK, (c + 1) * CHUNK, halo_part, 0)
        if c == 0:
            for side in range(2):

                @pl.when(z_receives[side])
                def _():
                    mean_copy(side).wait_recv()

        l, piece = c // per_level, c % per_level
        low = piece * CHUNK - (1 if piece else 0)
        high = rows if piece == per_level - 1 else (piece + 1) * CHUNK - 1
        lax.fori_loop(low, high, convert(l), 0)
        if piece == per_level - 1:
            part[t, l] = jnp.concatenate([sums[l * rows + j] for j in range(rows)], axis=0)
            for k in range(1, n_tm):
                part_copy(l, k, t).start()

            def narrow(s, carry):
                for h in range(2):
                    conv_ref[s, pl.ds(l * rows, rows), pl.ds(h * LANES, LANES)] = cf[
                        h, s, pl.ds(l * rows, rows), :
                    ].astype(jnp.bfloat16)
                return carry

            lax.fori_loop(0, snaps, narrow, 0)

    for l in range(levels):
        for k in range(1, n_tm):
            part_copy(l, k, lax.rem(t + n_tm - k, n_tm)).wait_recv()
        total = part[0, l]
        for s in range(1, n_tm):
            total = total + part[s, l]
        mean_ref[l] = total / (snaps * n_tm)

    for side in range(2):

        @pl.when(sends[side])
        def _():
            edge_copy(side).wait_send()
            for c in range(chunks):
                for f in range(2):
                    for h in range(2):
                        bulk(side, c, f, h).wait_send()

        @pl.when(z_sends[side])
        def _():
            mean_copy(side).wait_send()

    for l in range(levels):
        for k in range(1, n_tm):
            part_copy(l, k, t).wait_send()


def shards(velocity_u, velocity_v, land_sea, bottom_level, spacing_x, spacing_y):
    snaps, levels, rows, width = velocity_u.shape
    cells = levels * rows
    n_tm, n_tile = lax.axis_size("tm"), lax.axis_size("tile")
    assert width == 2 * LANES and 4 * cells == LANES and snaps >= HALF and rows % CHUNK == 0
    own, halo = band_parts(snaps)
    chunks = cells // CHUNK
    vmem = pl.BlockSpec(memory_space=pltpu.VMEM)
    anywhere = pl.BlockSpec(memory_space=pl.ANY)
    f32 = jnp.float32
    dma = pltpu.SemaphoreType.DMA
    conversion, mean_map = pl.pallas_call(
        functools.partial(kernel, n_tm, n_tile, levels),
        out_shape=(
            jax.ShapeDtypeStruct((snaps, cells, width), jnp.bfloat16),
            jax.ShapeDtypeStruct((levels, rows, width), f32),
        ),
        in_specs=[anywhere] * 2 + [vmem] * 6,
        out_specs=(vmem, vmem),
        scratch_shapes=[
            pltpu.VMEM((2, 2, snaps, cells, LANES), f32),
            pltpu.VMEM((2, 2, 2, HALF, cells, LANES), f32),
            pltpu.VMEM((2, levels, rows + 2, snaps, width), f32),
            pltpu.VMEM((2, snaps, cells, LANES), f32),
            pltpu.VMEM((cells, 1, width), f32),
            pltpu.VMEM((rows, 1, width), f32),
            pltpu.VMEM((rows, 1, width), f32),
            pltpu.VMEM((cells, 1, width), f32),
            pltpu.VMEM((n_tm, levels, rows, width), f32),
            pltpu.VMEM((snaps, LANES), f32),
            pltpu.VMEM((2, HALF, LANES), f32),
            pltpu.VMEM((snaps, LANES), f32),
            pltpu.VMEM((2, snaps, LANES), f32),
            dma((2, 2)),
            dma((2, chunks, 2, 2)),
            dma((2, chunks, 2, 2)),
            dma((2,)),
            dma((2,)),
            dma((2,)),
            dma((2,)),
            dma((levels, n_tm)),
            dma((levels, n_tm)),
        ],
        compiler_params=pltpu.CompilerParams(
            collective_id=0, has_side_effects=True, vmem_limit_bytes=40 * 1024 * 1024
        ),
        cost_estimate=pl.CostEstimate(flops=10**9, bytes_accessed=4 * 10**6, transcendentals=0),
    )(
        velocity_u.reshape(snaps, cells, width),
        velocity_v.reshape(snaps, cells, width),
        land_sea, bottom_level, spacing_x, spacing_y,
        jnp.asarray(own), jnp.asarray(halo),
    )
    return conversion.reshape(velocity_u.shape), mean_map


def solution(mesh):
    in_specs = (
        P("tm", None, None, "tile"),
        P("tm", None, None, "tile"),
        P(None, "tile"),
        P(None, "tile"),
        P(None, "tile"),
        P(None, "tile"),
    )
    out_specs = (P("tm", None, None, "tile"), P(None, None, "tile"))
    return jax.shard_map(shards, mesh=mesh, in_specs=in_specs, out_specs=out_specs, check_vma=False)
```

```python
import functools

import jax
import jax.numpy as jnp
import numpy as np
from jax import lax
from jax.experimental import pallas as pl
from jax.experimental.pallas import tpu as pltpu
from jax.sharding import PartitionSpec as P

HALF = 24
CUTOFF = 1.0 / 40.0
LANES = 128
CHUNK = 8
DEPTH = 2
UNROLL = 4
MESH = pl.DeviceIdType.MESH


def band_parts(count):
    offset = (np.arange(count + 2 * HALF)[None, :] - np.arange(count)[:, None] - HALF).astype(np.float64)
    weights = 2.0 * CUTOFF * np.sinc(2.0 * CUTOFF * offset) * np.sinc(offset / HALF)
    weights = np.where(np.abs(offset) <= HALF, weights, 0.0).astype(np.float32)
    own = weights[:, HALF : HALF + count]
    halo = np.concatenate([weights[:, :HALF], weights[:, HALF + count :]], axis=1)
    return own, halo


def dot(a, b):
    return jnp.dot(a, b, precision=lax.Precision.HIGHEST, preferred_element_type=jnp.float32)


def kernel(
    n_tm, n_tile, levels,
    u_ref, v_ref, land_in, bottom_in, sx_in, sy_in, own_in, halo_in,
    conv_ref, mean_ref,
    land_ref, bottom_ref, sx_ref, sy_ref, own_ref, halo_w_ref, small_sem,
    x, halo, mm, cf, wet, cx, cy, sums, part, edge, edge_halo, edge_mean, edge_in,
    x_sem, bulk_send, bulk_recv, edge_send, edge_recv, em_send, em_recv, part_send, part_recv,
):
    snaps, cells, width = u_ref.shape
    rows = cells // levels
    t = lax.axis_index("tm")
    z = lax.axis_index("tile")
    chunks = cells // CHUNK
    fields = (u_ref, v_ref)

    barrier = pltpu.get_barrier_semaphore()
    for k in range(1, n_tm):
        pl.semaphore_signal(barrier, inc=1, device_id={"tm": lax.rem(t + k, n_tm)}, device_id_type=MESH)

    @pl.when(z > 0)
    def _():
        pl.semaphore_signal(barrier, inc=1, device_id={"tile": z - 1}, device_id_type=MESH)

    @pl.when(z < n_tile - 1)
    def _():
        pl.semaphore_signal(barrier, inc=1, device_id={"tile": z + 1}, device_id_type=MESH)

    def local(f, h):
        return pltpu.make_async_copy(
            fields[f].at[:, :, pl.ds(h * LANES, LANES)], x.at[f, h], x_sem.at[f, h]
        )

    small = (
        (land_in, land_ref), (bottom_in, bottom_ref), (sx_in, sx_ref),
        (sy_in, sy_ref), (own_in, own_ref), (halo_in, halo_w_ref),
    )
    for i, (src, dst) in enumerate(small):
        pltpu.make_async_copy(src, dst, small_sem.at[i]).start()
    for f in range(2):
        for h in range(2):
            local(f, h).start()

    pl.semaphore_wait(barrier, n_tm - 1 + (z > 0).astype(jnp.int32) + (z < n_tile - 1).astype(jnp.int32))

    def bulk(side, c, f, h):
        first = snaps - HALF if side == 0 else 0
        to = t + 1 if side == 0 else t - 1
        return pltpu.make_async_remote_copy(
            src_ref=fields[f].at[pl.ds(first, HALF), pl.ds(c * CHUNK, CHUNK), pl.ds(h * LANES, LANES)],
            dst_ref=halo.at[side, f, h, :, pl.ds(c * CHUNK, CHUNK), :],
            send_sem=bulk_send.at[side, c, f, h],
            recv_sem=bulk_recv.at[side, c, f, h],
            device_id={"tm": to},
            device_id_type=MESH,
        )

    def edge_copy(side):
        first = snaps - HALF if side == 0 else 0
        to = t + 1 if side == 0 else t - 1
        return pltpu.make_async_remote_copy(
            src_ref=edge.at[pl.ds(first, HALF), :],
            dst_ref=edge_halo.at[side],
            send_sem=edge_send.at[side],
            recv_sem=edge_recv.at[side],
            device_id={"tm": to},
            device_id_type=MESH,
        )

    def mean_copy(side):
        to = z + 1 if side == 0 else z - 1
        return pltpu.make_async_remote_copy(
            src_ref=edge_mean,
            dst_ref=edge_in.at[side],
            send_sem=em_send.at[side],
            recv_sem=em_recv.at[side],
            device_id={"tile": to},
            device_id_type=MESH,
        )

    def part_copy(l, k, slot):
        return pltpu.make_async_remote_copy(
            src_ref=part.at[slot, l],
            dst_ref=part.at[slot, l],
            send_sem=part_send.at[l, k],
            recv_sem=part_recv.at[l, k],
            device_id={"tm": lax.rem(t + k, n_tm)},
            device_id_type=MESH,
        )

    sends = (t < n_tm - 1, t > 0)
    receives = (t > 0, t < n_tm - 1)
    z_sends = (z < n_tile - 1, z > 0)
    z_receives = (z > 0, z < n_tile - 1)

    def start_chunk(c):
        for side in range(2):

            @pl.when(sends[side])
            def _():
                for f in range(2):
                    for h in range(2):
                        bulk(side, c, f, h).start()

    def finish_chunk(c):
        for side in range(2):

            @pl.when(sends[side])
            def _():
                for f in range(2):
                    for h in range(2):
                        bulk(side, c, f, h).wait_send()

    for c in range(DEPTH):
        start_chunk(c)

    for side in range(2):

        @pl.when(jnp.logical_not(receives[side]))
        def _():
            halo[side] = jnp.zeros(halo.shape[1:], jnp.float32)
            edge_halo[side] = jnp.zeros(edge_halo.shape[1:], jnp.float32)

        @pl.when(jnp.logical_not(z_receives[side]))
        def _():
            edge_in[side] = jnp.zeros(edge_in.shape[1:], jnp.float32)

    for i, (src, dst) in enumerate(small):
        pltpu.make_async_copy(src, dst, small_sem.at[i]).wait()

    for l in range(levels):
        is_wet = (land_ref[...] == 1) & (l < bottom_ref[...])
        level_wet = jnp.where(is_wet, 1.0, 0.0).astype(jnp.float32)
        for j in range(rows):
            wet[l * rows + j] = level_wet[j : j + 1, :]
    all_x, all_y = 0.5 / sx_ref[...], 0.5 / sy_ref[...]
    for j in range(rows):
        cx[j] = all_x[j : j + 1, :]
        cy[j] = all_y[j : j + 1, :]
    for f in range(2):
        for l in range(levels):
            for j in (0, rows + 1):
                mm[f, l, j] = jnp.zeros((snaps, width), jnp.float32)
    column = lax.broadcasted_iota(jnp.int32, (snaps, 2 * HALF), 1)
    valid = ((column >= HALF) | (t > 0)) & ((column < HALF) | (t < n_tm - 1))
    own_w = own_ref[...]
    halo_w = jnp.where(valid, halo_w_ref[...], 0.0)
    weight_sum = jnp.sum(own_w, axis=1, keepdims=True) + jnp.sum(halo_w, axis=1, keepdims=True)
    own_w = own_w / weight_sum
    halo_w = halo_w / weight_sum

    for f in range(2):
        for h in range(2):
            local(f, h).wait()

    def series(ref, count, r):
        return ref.reshape(count * cells, LANES)[pl.ds(r, count, stride=cells), :]

    lane = lax.broadcasted_iota(jnp.int32, (snaps, LANES), 1)

    def pack(r, acc):
        for f in range(2):
            q = f * cells + r
            first = series(x.at[f, 0], snaps, r) * wet[r][:, :LANES]
            acc = jnp.where(lane == q, pltpu.roll(first, q, 1), acc)
            q = (2 + f) * cells + r
            last = series(x.at[f, 1], snaps, r) * wet[r][:, width - LANES :]
            acc = jnp.where(lane == q, pltpu.roll(last, lax.rem(q + 1, LANES), 1), acc)
        return acc

    edge[...] = lax.fori_loop(0, cells, pack, jnp.zeros((snaps, LANES), jnp.float32))
    for side in range(2):

        @pl.when(sends[side])
        def _():
            edge_copy(side).start()

    def own_part(r, carry):
        l, j = r // rows, lax.rem(r, rows)
        for f in range(2):
            block = jnp.concatenate([series(x.at[f, h], snaps, r) for h in range(2)], axis=1)
            mm[f, l, j + 1] = dot(own_w, block)
        return carry

    lax.fori_loop(0, cells, own_part, 0, unroll=UNROLL)

    for side in range(2):

        @pl.when(receives[side])
        def _():
            edge_copy(side).wait_recv()

    edge_mean[...] = dot(own_w, edge[...]) + dot(
        halo_w, jnp.concatenate([edge_halo[0], edge_halo[1]], axis=0)
    )
    for side in range(2):

        @pl.when(z_sends[side])
        def _():
            mean_copy(side).start()

    wide = lax.broadcasted_iota(jnp.int32, (snaps, width), 1)

    def halo_part(r, carry):
        l, j = r // rows, lax.rem(r, rows)
        mask = wet[r]
        for f in range(2):
            block = jnp.concatenate(
                [
                    jnp.concatenate([series(halo.at[s, f, h], HALF, r) for h in range(2)], axis=1)
                    for s in range(2)
                ],
                axis=0,
            )
            mm[f, l, j + 1] = (mm[f, l, j + 1] + dot(halo_w, block)) * mask
        return carry

    def grad_x(f, r, masked, scale):
        q = (2 + f) * cells + r
        before = pltpu.roll(edge_in[0], lax.rem(2 * LANES - q, LANES), 1)
        q = f * cells + r
        after = pltpu.roll(edge_in[1], lax.rem(2 * LANES - 1 - q, LANES), 1)
        before = jnp.concatenate([before, before], axis=1)
        after = jnp.concatenate([after, after], axis=1)
        behind = jnp.where(wide == 0, before, pltpu.roll(masked, 1, 1))
        ahead = jnp.where(wide == width - 1, after, pltpu.roll(masked, width - 1, 1))
        return (ahead - behind) * scale

    def convert(l):
        def body(j, carry):
            r = l * rows + j
            mask = wet[r]
            scale_x = cx[j]
            scale_y = cy[j]
            eddy, gx, gy = [], [], []
            for f in range(2):
                masked = mm[f, l, j + 1]
                raw = jnp.concatenate([series(x.at[f, h], snaps, r) for h in range(2)], axis=1)
                eddy.append(raw - masked)
                gx.append(grad_x(f, r, masked, scale_x))
                gy.append((mm[f, l, j + 2] - mm[f, l, j]) * scale_y)
            eu, ev = eddy
            total = eu * eu * gx[0] + eu * ev * (gy[0] + gx[1]) + ev * ev * gy[1]
            conversion = -mask * total
            for h in range(2):
                cf.at[h].reshape(snaps * cells, LANES)[pl.ds(r, snaps, stride=cells), :] = conversion[
                    :, h * LANES : (h + 1) * LANES
                ]
            sums[r] = jnp.sum(conversion, axis=0, keepdims=True)
            return carry

        return body

    per_level = rows // CHUNK
    for c in range(chunks):
        finish_chunk(c)
        if c + DEPTH < chunks:
            start_chunk(c + DEPTH)
        for side in range(2):

            @pl.when(receives[side])
            def _():
                for f in range(2):
                    for h in range(2):
                        bulk(side, c, f, h).wait_recv()

        lax.fori_loop(c * CHUNK, (c + 1) * CHUNK, halo_part, 0, unroll=UNROLL)
        if c == 0:
            for side in range(2):

                @pl.when(z_receives[side])
                def _():
                    mean_copy(side).wait_recv()

        l, piece = c // per_level, c % per_level
        low = piece * CHUNK - (1 if piece else 0)
        high = rows if piece == per_level - 1 else (piece + 1) * CHUNK - 1
        lax.fori_loop(low, high, convert(l), 0)
        if piece == per_level - 1:
            part[t, l] = jnp.concatenate([sums[l * rows + j] for j in range(rows)], axis=0)
            for k in range(1, n_tm):
                part_copy(l, k, t).start()

            def narrow(s, carry):
                for h in range(2):
                    conv_ref[s, pl.ds(l * rows, rows), pl.ds(h * LANES, LANES)] = cf[
                        h, s, pl.ds(l * rows, rows), :
                    ].astype(jnp.bfloat16)
                return carry

            lax.fori_loop(0, snaps, narrow, 0)

    for l in range(levels):
        for k in range(1, n_tm):
            part_copy(l, k, lax.rem(t + n_tm - k, n_tm)).wait_recv()
        total = part[0, l]
        for s in range(1, n_tm):
            total = total + part[s, l]
        mean_ref[l] = total / (snaps * n_tm)

    for side in range(2):

        @pl.when(sends[side])
        def _():
            edge_copy(side).wait_send()

        @pl.when(z_sends[side])
        def _():
            mean_copy(side).wait_send()

    for l in range(levels):
        for k in range(1, n_tm):
            part_copy(l, k, t).wait_send()


def shards(velocity_u, velocity_v, land_sea, bottom_level, spacing_x, spacing_y):
    snaps, levels, rows, width = velocity_u.shape
    cells = levels * rows
    n_tm, n_tile = lax.axis_size("tm"), lax.axis_size("tile")
    assert width == 2 * LANES and 4 * cells == LANES and snaps >= HALF and rows % CHUNK == 0
    own, halo = band_parts(snaps)
    chunks = cells // CHUNK
    vmem = pl.BlockSpec(memory_space=pltpu.VMEM)
    hbm = pl.BlockSpec(memory_space=pltpu.HBM)
    f32 = jnp.float32
    dma = pltpu.SemaphoreType.DMA
    conversion, mean_map = pl.pallas_call(
        functools.partial(kernel, n_tm, n_tile, levels),
        out_shape=(
            jax.ShapeDtypeStruct((snaps, cells, width), jnp.bfloat16),
            jax.ShapeDtypeStruct((levels, rows, width), f32),
        ),
        in_specs=[hbm] * 8,
        out_specs=(vmem, vmem),
        scratch_shapes=[
            pltpu.VMEM((rows, width), jnp.int32),
            pltpu.VMEM((rows, width), jnp.int32),
            pltpu.VMEM((rows, width), f32),
            pltpu.VMEM((rows, width), f32),
            pltpu.VMEM(own.shape, f32),
            pltpu.VMEM(halo.shape, f32),
            dma((6,)),
            pltpu.VMEM((2, 2, snaps, cells, LANES), f32),
            pltpu.VMEM((2, 2, 2, HALF, cells, LANES), f32),
            pltpu.VMEM((2, levels, rows + 2, snaps, width), f32),
            pltpu.VMEM((2, snaps, cells, LANES), f32),
            pltpu.VMEM((cells, 1, width), f32),
            pltpu.VMEM((rows, 1, width), f32),
            pltpu.VMEM((rows, 1, width), f32),
            pltpu.VMEM((cells, 1, width), f32),
            pltpu.VMEM((n_tm, levels, rows, width), f32),
            pltpu.VMEM((snaps, LANES), f32),
            pltpu.VMEM((2, HALF, LANES), f32),
            pltpu.VMEM((snaps, LANES), f32),
            pltpu.VMEM((2, snaps, LANES), f32),
            dma((2, 2)),
            dma((2, chunks, 2, 2)),
            dma((2, chunks, 2, 2)),
            dma((2,)),
            dma((2,)),
            dma((2,)),
            dma((2,)),
            dma((levels, n_tm)),
            dma((levels, n_tm)),
        ],
        compiler_params=pltpu.CompilerParams(
            collective_id=0, has_side_effects=True, vmem_limit_bytes=40 * 1024 * 1024
        ),
        cost_estimate=pl.CostEstimate(flops=10**9, bytes_accessed=4 * 10**6, transcendentals=0),
    )(
        velocity_u.reshape(snaps, cells, width),
        velocity_v.reshape(snaps, cells, width),
        land_sea, bottom_level, spacing_x, spacing_y,
        jnp.asarray(own), jnp.asarray(halo),
    )
    return conversion.reshape(velocity_u.shape), mean_map


def solution(mesh):
    in_specs = (
        P("tm", None, None, "tile"),
        P("tm", None, None, "tile"),
        P(None, "tile"),
        P(None, "tile"),
        P(None, "tile"),
        P(None, "tile"),
    )
    out_specs = (P("tm", None, None, "tile"), P(None, None, "tile"))
    return jax.shard_map(shards, mesh=mesh, in_specs=in_specs, out_specs=out_specs, check_vma=False)
```

```python
import functools

import jax
import jax.numpy as jnp
import numpy as np
from jax import lax
from jax.experimental import pallas as pl
from jax.experimental.pallas import tpu as pltpu
from jax.sharding import PartitionSpec as P

HALF = 24
CUTOFF = 1.0 / 40.0
LANES = 128
CHUNK = 8
DEPTH = 2
UNROLL = 4
MESH = pl.DeviceIdType.MESH


def band_parts(count):
    offset = (np.arange(count + 2 * HALF)[None, :] - np.arange(count)[:, None] - HALF).astype(np.float64)
    weights = 2.0 * CUTOFF * np.sinc(2.0 * CUTOFF * offset) * np.sinc(offset / HALF)
    weights = np.where(np.abs(offset) <= HALF, weights, 0.0).astype(np.float32)
    own = weights[:, HALF : HALF + count]
    halo = np.concatenate([weights[:, :HALF], weights[:, HALF + count :]], axis=1)
    return own, halo


def dot(a, b):
    return jnp.dot(a, b, precision=lax.Precision.HIGHEST, preferred_element_type=jnp.float32)


def kernel(
    n_tm, n_tile, levels,
    u_ref, v_ref, land_in, bottom_in, sx_in, sy_in, own_in, halo_in,
    conv_ref, mean_ref,
    land_ref, bottom_ref, sx_ref, sy_ref, own_ref, halo_w_ref, small_sem,
    x, halo, mm, cf, wet, cx, cy, sums, part, edge, edge_halo, edge_mean, edge_in,
    relayed, relay_send, relay_recv,
    x_sem, bulk_send, bulk_recv, edge_send, edge_recv, em_send, em_recv, part_send, part_recv,
):
    snaps, cells, width = u_ref.shape
    rows = cells // levels
    t = lax.axis_index("tm")
    z = lax.axis_index("tile")
    chunks = cells // CHUNK
    fields = (u_ref, v_ref)

    barrier = pltpu.get_barrier_semaphore()
    for k in range(1, n_tm):
        pl.semaphore_signal(barrier, inc=1, device_id={"tm": lax.rem(t + k, n_tm)}, device_id_type=MESH)

    @pl.when(z > 0)
    def _():
        pl.semaphore_signal(barrier, inc=1, device_id={"tile": z - 1}, device_id_type=MESH)

    @pl.when(z < n_tile - 1)
    def _():
        pl.semaphore_signal(barrier, inc=1, device_id={"tile": z + 1}, device_id_type=MESH)

    def local(f, h):
        return pltpu.make_async_copy(
            fields[f].at[:, :, pl.ds(h * LANES, LANES)], x.at[f, h], x_sem.at[f, h]
        )

    small = (
        (land_in, land_ref), (bottom_in, bottom_ref), (sx_in, sx_ref),
        (sy_in, sy_ref), (own_in, own_ref), (halo_in, halo_w_ref),
    )
    for i, (src, dst) in enumerate(small):
        pltpu.make_async_copy(src, dst, small_sem.at[i]).start()
    for f in range(2):
        for h in range(2):
            local(f, h).start()

    pl.semaphore_wait(barrier, n_tm - 1 + (z > 0).astype(jnp.int32) + (z < n_tile - 1).astype(jnp.int32))

    def bulk(side, c, f, h):
        first = snaps - HALF if side == 0 else 0
        to = t + 1 if side == 0 else t - 1
        return pltpu.make_async_remote_copy(
            src_ref=fields[f].at[pl.ds(first, HALF), pl.ds(c * CHUNK, CHUNK), pl.ds(h * LANES, LANES)],
            dst_ref=halo.at[side, f, h, :, pl.ds(c * CHUNK, CHUNK), :],
            send_sem=bulk_send.at[side, c, f, h],
            recv_sem=bulk_recv.at[side, c, f, h],
            device_id={"tm": to},
            device_id_type=MESH,
        )

    middle = (n_tm // 2 - 1, n_tm // 2)
    via = (n_tm - 1, 0)

    def to_relay(side, c, h):
        first = snaps - HALF if side == 0 else 0
        return pltpu.make_async_remote_copy(
            src_ref=fields[1].at[pl.ds(first, HALF), pl.ds(c * CHUNK, CHUNK), pl.ds(h * LANES, LANES)],
            dst_ref=relayed.at[c, h],
            send_sem=bulk_send.at[side, c, 1, h],
            recv_sem=relay_recv.at[c, h],
            device_id={"tm": via[side]},
            device_id_type=MESH,
        )

    def from_relay(side, c, h):
        return pltpu.make_async_remote_copy(
            src_ref=relayed.at[c, h],
            dst_ref=halo.at[side, 1, h, :, pl.ds(c * CHUNK, CHUNK), :],
            send_sem=relay_send.at[c, h],
            recv_sem=bulk_recv.at[side, c, 1, h],
            device_id={"tm": middle[1 - side]},
            device_id_type=MESH,
        )

    def pass_on(c):
        if n_tm < 4:
            return
        for side in range(2):

            @pl.when(t == via[side])
            def _():
                for h in range(2):
                    to_relay(side, c, h).wait_recv()
                    from_relay(side, c, h).start()

    def edge_copy(side):
        first = snaps - HALF if side == 0 else 0
        to = t + 1 if side == 0 else t - 1
        return pltpu.make_async_remote_copy(
            src_ref=edge.at[pl.ds(first, HALF), :],
            dst_ref=edge_halo.at[side],
            send_sem=edge_send.at[side],
            recv_sem=edge_recv.at[side],
            device_id={"tm": to},
            device_id_type=MESH,
        )

    def mean_copy(side):
        to = z + 1 if side == 0 else z - 1
        return pltpu.make_async_remote_copy(
            src_ref=edge_mean,
            dst_ref=edge_in.at[side],
            send_sem=em_send.at[side],
            recv_sem=em_recv.at[side],
            device_id={"tile": to},
            device_id_type=MESH,
        )

    def part_copy(l, k, slot):
        return pltpu.make_async_remote_copy(
            src_ref=part.at[slot, l],
            dst_ref=part.at[slot, l],
            send_sem=part_send.at[l, k],
            recv_sem=part_recv.at[l, k],
            device_id={"tm": lax.rem(t + k, n_tm)},
            device_id_type=MESH,
        )

    sends = (t < n_tm - 1, t > 0)
    receives = (t > 0, t < n_tm - 1)
    z_sends = (z < n_tile - 1, z > 0)
    z_receives = (z > 0, z < n_tile - 1)

    def start_chunk(c):
        for side in range(2):

            if n_tm >= 4:

                @pl.when(t == middle[side])
                def _():
                    for h in range(2):
                        to_relay(side, c, h).start()
                        bulk(side, c, 0, h).start()

                whole = sends[side] & (t != middle[side])
            else:
                whole = sends[side]

            @pl.when(whole)
            def _():
                for f in range(2):
                    for h in range(2):
                        bulk(side, c, f, h).start()

    def finish_chunk(c):
        for side in range(2):

            @pl.when(sends[side])
            def _():
                for f in range(2):
                    for h in range(2):
                        bulk(side, c, f, h).wait_send()

    for c in range(DEPTH):
        start_chunk(c)

    for side in range(2):

        @pl.when(jnp.logical_not(receives[side]))
        def _():
            halo[side] = jnp.zeros(halo.shape[1:], jnp.float32)
            edge_halo[side] = jnp.zeros(edge_halo.shape[1:], jnp.float32)

        @pl.when(jnp.logical_not(z_receives[side]))
        def _():
            edge_in[side] = jnp.zeros(edge_in.shape[1:], jnp.float32)

    for i, (src, dst) in enumerate(small):
        pltpu.make_async_copy(src, dst, small_sem.at[i]).wait()

    for l in range(levels):
        is_wet = (land_ref[...] == 1) & (l < bottom_ref[...])
        level_wet = jnp.where(is_wet, 1.0, 0.0).astype(jnp.float32)
        for j in range(rows):
            wet[l * rows + j] = level_wet[j : j + 1, :]
    all_x, all_y = 0.5 / sx_ref[...], 0.5 / sy_ref[...]
    for j in range(rows):
        cx[j] = all_x[j : j + 1, :]
        cy[j] = all_y[j : j + 1, :]
    for f in range(2):
        for l in range(levels):
            for j in (0, rows + 1):
                mm[f, l, j] = jnp.zeros((snaps, width), jnp.float32)
    column = lax.broadcasted_iota(jnp.int32, (snaps, 2 * HALF), 1)
    valid = ((column >= HALF) | (t > 0)) & ((column < HALF) | (t < n_tm - 1))
    own_w = own_ref[...]
    halo_w = jnp.where(valid, halo_w_ref[...], 0.0)
    weight_sum = jnp.sum(own_w, axis=1, keepdims=True) + jnp.sum(halo_w, axis=1, keepdims=True)
    own_w = own_w / weight_sum
    halo_w = halo_w / weight_sum

    for f in range(2):
        for h in range(2):
            local(f, h).wait()

    def series(ref, count, r):
        return ref.reshape(count * cells, LANES)[pl.ds(r, count, stride=cells), :]

    lane = lax.broadcasted_iota(jnp.int32, (snaps, LANES), 1)

    def pack(r, acc):
        for f in range(2):
            q = f * cells + r
            first = series(x.at[f, 0], snaps, r) * wet[r][:, :LANES]
            acc = jnp.where(lane == q, pltpu.roll(first, q, 1), acc)
            q = (2 + f) * cells + r
            last = series(x.at[f, 1], snaps, r) * wet[r][:, width - LANES :]
            acc = jnp.where(lane == q, pltpu.roll(last, lax.rem(q + 1, LANES), 1), acc)
        return acc

    edge[...] = lax.fori_loop(0, cells, pack, jnp.zeros((snaps, LANES), jnp.float32), unroll=UNROLL)
    for side in range(2):

        @pl.when(sends[side])
        def _():
            edge_copy(side).start()

    pass_on(0)

    def own_part(r, carry):
        l, j = r // rows, lax.rem(r, rows)
        for f in range(2):
            block = jnp.concatenate([series(x.at[f, h], snaps, r) for h in range(2)], axis=1)
            mm[f, l, j + 1] = dot(own_w, block)
        return carry

    lax.fori_loop(0, cells, own_part, 0, unroll=UNROLL)
    for c in range(1, DEPTH):
        pass_on(c)

    for side in range(2):

        @pl.when(receives[side])
        def _():
            edge_copy(side).wait_recv()

    edge_mean[...] = dot(own_w, edge[...]) + dot(
        halo_w, jnp.concatenate([edge_halo[0], edge_halo[1]], axis=0)
    )
    for side in range(2):

        @pl.when(z_sends[side])
        def _():
            mean_copy(side).start()

    wide = lax.broadcasted_iota(jnp.int32, (snaps, width), 1)

    def halo_part(r, carry):
        l, j = r // rows, lax.rem(r, rows)
        mask = wet[r]
        for f in range(2):
            block = jnp.concatenate(
                [
                    jnp.concatenate([series(halo.at[s, f, h], HALF, r) for h in range(2)], axis=1)
                    for s in range(2)
                ],
                axis=0,
            )
            mm[f, l, j + 1] = (mm[f, l, j + 1] + dot(halo_w, block)) * mask
        return carry

    def grad_x(f, r, masked, scale):
        q = (2 + f) * cells + r
        before = pltpu.roll(edge_in[0], lax.rem(2 * LANES - q, LANES), 1)
        q = f * cells + r
        after = pltpu.roll(edge_in[1], lax.rem(2 * LANES - 1 - q, LANES), 1)
        before = jnp.concatenate([before, before], axis=1)
        after = jnp.concatenate([after, after], axis=1)
        behind = jnp.where(wide == 0, before, pltpu.roll(masked, 1, 1))
        ahead = jnp.where(wide == width - 1, after, pltpu.roll(masked, width - 1, 1))
        return (ahead - behind) * scale

    def convert(l):
        def body(j, carry):
            r = l * rows + j
            mask = wet[r]
            scale_x = cx[j]
            scale_y = cy[j]
            eddy, gx, gy = [], [], []
            for f in range(2):
                masked = mm[f, l, j + 1]
                raw = jnp.concatenate([series(x.at[f, h], snaps, r) for h in range(2)], axis=1)
                eddy.append(raw - masked)
                gx.append(grad_x(f, r, masked, scale_x))
                gy.append((mm[f, l, j + 2] - mm[f, l, j]) * scale_y)
            eu, ev = eddy
            total = eu * eu * gx[0] + eu * ev * (gy[0] + gx[1]) + ev * ev * gy[1]
            conversion = -mask * total
            for h in range(2):
                cf.at[h].reshape(snaps * cells, LANES)[pl.ds(r, snaps, stride=cells), :] = conversion[
                    :, h * LANES : (h + 1) * LANES
                ]
            sums[r] = jnp.sum(conversion, axis=0, keepdims=True)
            return carry

        return body

    per_level = rows // CHUNK
    for c in range(chunks):
        finish_chunk(c)
        if c + DEPTH < chunks:
            start_chunk(c + DEPTH)
        for side in range(2):

            @pl.when(receives[side])
            def _():
                for f in range(2):
                    for h in range(2):
                        bulk(side, c, f, h).wait_recv()

        lax.fori_loop(c * CHUNK, (c + 1) * CHUNK, halo_part, 0, unroll=UNROLL)
        if c == 0:
            for side in range(2):

                @pl.when(z_receives[side])
                def _():
                    mean_copy(side).wait_recv()

        l, piece = c // per_level, c % per_level
        low = piece * CHUNK - (1 if piece else 0)
        high = rows if piece == per_level - 1 else (piece + 1) * CHUNK - 1
        lax.fori_loop(low, high, convert(l), 0, unroll=2)
        if c + DEPTH < chunks:
            pass_on(c + DEPTH)
        if piece == per_level - 1:
            part[t, l] = jnp.concatenate([sums[l * rows + j] for j in range(rows)], axis=0)
            for k in range(1, n_tm):
                part_copy(l, k, t).start()

            def narrow(s, carry):
                for h in range(2):
                    conv_ref[s, pl.ds(l * rows, rows), pl.ds(h * LANES, LANES)] = cf[
                        h, s, pl.ds(l * rows, rows), :
                    ].astype(jnp.bfloat16)
                return carry

            lax.fori_loop(0, snaps, narrow, 0)

    for l in range(levels):
        for k in range(1, n_tm):
            part_copy(l, k, lax.rem(t + n_tm - k, n_tm)).wait_recv()
        total = part[0, l]
        for s in range(1, n_tm):
            total = total + part[s, l]
        mean_ref[l] = total / (snaps * n_tm)

    for side in range(2):

        @pl.when(sends[side])
        def _():
            edge_copy(side).wait_send()

        @pl.when(z_sends[side])
        def _():
            mean_copy(side).wait_send()

        if n_tm >= 4:

            @pl.when(t == via[side])
            def _():
                for c in range(chunks):
                    for h in range(2):
                        from_relay(side, c, h).wait_send()

    for l in range(levels):
        for k in range(1, n_tm):
            part_copy(l, k, t).wait_send()


def shards(velocity_u, velocity_v, land_sea, bottom_level, spacing_x, spacing_y):
    snaps, levels, rows, width = velocity_u.shape
    cells = levels * rows
    n_tm, n_tile = lax.axis_size("tm"), lax.axis_size("tile")
    assert width == 2 * LANES and 4 * cells == LANES and snaps >= HALF and rows % CHUNK == 0
    own, halo = band_parts(snaps)
    chunks = cells // CHUNK
    vmem = pl.BlockSpec(memory_space=pltpu.VMEM)
    hbm = pl.BlockSpec(memory_space=pltpu.HBM)
    f32 = jnp.float32
    dma = pltpu.SemaphoreType.DMA
    conversion, mean_map = pl.pallas_call(
        functools.partial(kernel, n_tm, n_tile, levels),
        out_shape=(
            jax.ShapeDtypeStruct((snaps, cells, width), jnp.bfloat16),
            jax.ShapeDtypeStruct((levels, rows, width), f32),
        ),
        in_specs=[hbm] * 8,
        out_specs=(vmem, vmem),
        scratch_shapes=[
            pltpu.VMEM((rows, width), jnp.int32),
            pltpu.VMEM((rows, width), jnp.int32),
            pltpu.VMEM((rows, width), f32),
            pltpu.VMEM((rows, width), f32),
            pltpu.VMEM(own.shape, f32),
            pltpu.VMEM(halo.shape, f32),
            dma((6,)),
            pltpu.VMEM((2, 2, snaps, cells, LANES), f32),
            pltpu.VMEM((2, 2, 2, HALF, cells, LANES), f32),
            pltpu.VMEM((2, levels, rows + 2, snaps, width), f32),
            pltpu.VMEM((2, snaps, cells, LANES), f32),
            pltpu.VMEM((cells, 1, width), f32),
            pltpu.VMEM((rows, 1, width), f32),
            pltpu.VMEM((rows, 1, width), f32),
            pltpu.VMEM((cells, 1, width), f32),
            pltpu.VMEM((n_tm, levels, rows, width), f32),
            pltpu.VMEM((snaps, LANES), f32),
            pltpu.VMEM((2, HALF, LANES), f32),
            pltpu.VMEM((snaps, LANES), f32),
            pltpu.VMEM((2, snaps, LANES), f32),
            pltpu.VMEM((chunks, 2, HALF, CHUNK, LANES), f32),
            dma((chunks, 2)),
            dma((chunks, 2)),
            dma((2, 2)),
            dma((2, chunks, 2, 2)),
            dma((2, chunks, 2, 2)),
            dma((2,)),
            dma((2,)),
            dma((2,)),
            dma((2,)),
            dma((levels, n_tm)),
            dma((levels, n_tm)),
        ],
        compiler_params=pltpu.CompilerParams(
            collective_id=0, has_side_effects=True, vmem_limit_bytes=40 * 1024 * 1024
        ),
        cost_estimate=pl.CostEstimate(flops=10**9, bytes_accessed=4 * 10**6, transcendentals=0),
    )(
        velocity_u.reshape(snaps, cells, width),
        velocity_v.reshape(snaps, cells, width),
        land_sea, bottom_level, spacing_x, spacing_y,
        jnp.asarray(own), jnp.asarray(halo),
    )
    return conversion.reshape(velocity_u.shape), mean_map


def solution(mesh):
    in_specs = (
        P("tm", None, None, "tile"),
        P("tm", None, None, "tile"),
        P(None, "tile"),
        P(None, "tile"),
        P(None, "tile"),
        P(None, "tile"),
    )
    out_specs = (P("tm", None, None, "tile"), P(None, None, "tile"))
    return jax.shard_map(shards, mesh=mesh, in_specs=in_specs, out_specs=out_specs, check_vma=False)
```

```python
import functools

import jax
import jax.numpy as jnp
import numpy as np
from jax import lax
from jax.experimental import pallas as pl
from jax.experimental.pallas import tpu as pltpu
from jax.sharding import PartitionSpec as P

HALF = 24
CUTOFF = 1.0 / 40.0
LANES = 128
CHUNK = 8
DEPTH = 2
UNROLL = 4
MESH = pl.DeviceIdType.MESH


def band_parts(count):
    offset = (np.arange(count + 2 * HALF)[None, :] - np.arange(count)[:, None] - HALF).astype(np.float64)
    weights = 2.0 * CUTOFF * np.sinc(2.0 * CUTOFF * offset) * np.sinc(offset / HALF)
    weights = np.where(np.abs(offset) <= HALF, weights, 0.0).astype(np.float32)
    own = weights[:, HALF : HALF + count]
    halo = np.concatenate([weights[:, :HALF], weights[:, HALF + count :]], axis=1)
    return own, halo


def dot(a, b):
    return jnp.dot(a, b, precision=lax.Precision.HIGHEST, preferred_element_type=jnp.float32)


def kernel(
    n_tm, n_tile, levels,
    u_ref, v_ref, land_in, bottom_in, sx_in, sy_in, own_in, halo_in,
    conv_ref, mean_ref,
    land_ref, bottom_ref, sx_ref, sy_ref, own_ref, halo_w_ref, small_sem,
    x, halo, mm, cf, wet, cx, cy, sums, part, edge, edge_halo, edge_mean, edge_in,
    relayed, relay_send, relay_recv,
    x_sem, bulk_send, bulk_recv, edge_send, edge_recv, em_send, em_recv, part_send, part_recv,
):
    snaps, cells, width = u_ref.shape
    rows = cells // levels
    t = lax.axis_index("tm")
    z = lax.axis_index("tile")
    chunks = cells // CHUNK
    fields = (u_ref, v_ref)

    barrier = pltpu.get_barrier_semaphore()
    for k in range(1, n_tm):
        pl.semaphore_signal(barrier, inc=1, device_id={"tm": lax.rem(t + k, n_tm)}, device_id_type=MESH)

    @pl.when(z > 0)
    def _():
        pl.semaphore_signal(barrier, inc=1, device_id={"tile": z - 1}, device_id_type=MESH)

    @pl.when(z < n_tile - 1)
    def _():
        pl.semaphore_signal(barrier, inc=1, device_id={"tile": z + 1}, device_id_type=MESH)

    def local(f, h):
        return pltpu.make_async_copy(
            fields[f].at[:, :, pl.ds(h * LANES, LANES)], x.at[f, h], x_sem.at[f, h]
        )

    small = (
        (land_in, land_ref), (bottom_in, bottom_ref), (sx_in, sx_ref),
        (sy_in, sy_ref), (own_in, own_ref), (halo_in, halo_w_ref),
    )
    for i, (src, dst) in enumerate(small):
        pltpu.make_async_copy(src, dst, small_sem.at[i]).start()
    for f in range(2):
        for h in range(2):
            local(f, h).start()

    pl.semaphore_wait(barrier, n_tm - 1 + (z > 0).astype(jnp.int32) + (z < n_tile - 1).astype(jnp.int32))

    def bulk(side, c, f, h):
        first = snaps - HALF if side == 0 else 0
        to = t + 1 if side == 0 else t - 1
        return pltpu.make_async_remote_copy(
            src_ref=fields[f].at[pl.ds(first, HALF), pl.ds(c * CHUNK, CHUNK), pl.ds(h * LANES, LANES)],
            dst_ref=halo.at[side, f, h, :, pl.ds(c * CHUNK, CHUNK), :],
            send_sem=bulk_send.at[side, c, f, h],
            recv_sem=bulk_recv.at[side, c, f, h],
            device_id={"tm": to},
            device_id_type=MESH,
        )

    middle = (n_tm // 2 - 1, n_tm // 2)
    via = (n_tm - 1, 0)

    def to_relay(side, c, h):
        first = snaps - HALF if side == 0 else 0
        return pltpu.make_async_remote_copy(
            src_ref=fields[1].at[pl.ds(first, HALF), pl.ds(c * CHUNK, CHUNK), pl.ds(h * LANES, LANES)],
            dst_ref=relayed.at[c, h],
            send_sem=bulk_send.at[side, c, 1, h],
            recv_sem=relay_recv.at[c, h],
            device_id={"tm": via[side]},
            device_id_type=MESH,
        )

    def from_relay(side, c, h):
        return pltpu.make_async_remote_copy(
            src_ref=relayed.at[c, h],
            dst_ref=halo.at[side, 1, h, :, pl.ds(c * CHUNK, CHUNK), :],
            send_sem=relay_send.at[c, h],
            recv_sem=bulk_recv.at[side, c, 1, h],
            device_id={"tm": middle[1 - side]},
            device_id_type=MESH,
        )

    def pass_on(c):
        if n_tm < 4:
            return
        for side in range(2):

            @pl.when(t == via[side])
            def _():
                for h in range(2):
                    to_relay(side, c, h).wait_recv()
                    from_relay(side, c, h).start()

    def edge_copy(side):
        first = snaps - HALF if side == 0 else 0
        to = t + 1 if side == 0 else t - 1
        return pltpu.make_async_remote_copy(
            src_ref=edge.at[pl.ds(first, HALF), :],
            dst_ref=edge_halo.at[side],
            send_sem=edge_send.at[side],
            recv_sem=edge_recv.at[side],
            device_id={"tm": to},
            device_id_type=MESH,
        )

    def mean_copy(side):
        to = z + 1 if side == 0 else z - 1
        return pltpu.make_async_remote_copy(
            src_ref=edge_mean,
            dst_ref=edge_in.at[side],
            send_sem=em_send.at[side],
            recv_sem=em_recv.at[side],
            device_id={"tile": to},
            device_id_type=MESH,
        )

    def part_copy(l, k, slot):
        return pltpu.make_async_remote_copy(
            src_ref=part.at[slot, l],
            dst_ref=part.at[slot, l],
            send_sem=part_send.at[l, k],
            recv_sem=part_recv.at[l, k],
            device_id={"tm": lax.rem(t + k, n_tm)},
            device_id_type=MESH,
        )

    sends = (t < n_tm - 1, t > 0)
    receives = (t > 0, t < n_tm - 1)
    z_sends = (z < n_tile - 1, z > 0)
    z_receives = (z > 0, z < n_tile - 1)

    def start_chunk(c):
        for side in range(2):

            if n_tm >= 4:

                @pl.when(t == middle[side])
                def _():
                    for h in range(2):
                        to_relay(side, c, h).start()
                        bulk(side, c, 0, h).start()

                whole = sends[side] & (t != middle[side])
            else:
                whole = sends[side]

            @pl.when(whole)
            def _():
                for f in range(2):
                    for h in range(2):
                        bulk(side, c, f, h).start()

    def finish_chunk(c):
        for side in range(2):

            @pl.when(sends[side])
            def _():
                for f in range(2):
                    for h in range(2):
                        bulk(side, c, f, h).wait_send()

    for c in range(DEPTH):
        start_chunk(c)

    for side in range(2):

        @pl.when(jnp.logical_not(receives[side]))
        def _():
            halo[side] = jnp.zeros(halo.shape[1:], jnp.float32)
            edge_halo[side] = jnp.zeros(edge_halo.shape[1:], jnp.float32)

        @pl.when(jnp.logical_not(z_receives[side]))
        def _():
            edge_in[side] = jnp.zeros(edge_in.shape[1:], jnp.float32)

    for i, (src, dst) in enumerate(small):
        pltpu.make_async_copy(src, dst, small_sem.at[i]).wait()

    for l in range(levels):
        is_wet = (land_ref[...] == 1) & (l < bottom_ref[...])
        level_wet = jnp.where(is_wet, 1.0, 0.0).astype(jnp.float32)
        for j in range(rows):
            wet[l * rows + j] = level_wet[j : j + 1, :]
    all_x, all_y = 0.5 / sx_ref[...], 0.5 / sy_ref[...]
    for j in range(rows):
        cx[j] = all_x[j : j + 1, :]
        cy[j] = all_y[j : j + 1, :]
    for f in range(2):
        for l in range(levels):
            for j in (0, rows + 1):
                mm[f, l, j] = jnp.zeros((snaps, width), jnp.float32)
    column = lax.broadcasted_iota(jnp.int32, (snaps, 2 * HALF), 1)
    valid = ((column >= HALF) | (t > 0)) & ((column < HALF) | (t < n_tm - 1))
    own_w = own_ref[...]
    halo_w = jnp.where(valid, halo_w_ref[...], 0.0)
    weight_sum = jnp.sum(own_w, axis=1, keepdims=True) + jnp.sum(halo_w, axis=1, keepdims=True)
    own_w = own_w / weight_sum
    halo_w = halo_w / weight_sum

    for f in range(2):
        for h in range(2):
            local(f, h).wait()

    def series(ref, count, r):
        return ref.reshape(count * cells, LANES)[pl.ds(r, count, stride=cells), :]

    lane = lax.broadcasted_iota(jnp.int32, (snaps, LANES), 1)

    def pack(r, acc):
        for f in range(2):
            q = f * cells + r
            first = series(x.at[f, 0], snaps, r) * wet[r][:, :LANES]
            acc = jnp.where(lane == q, pltpu.roll(first, q, 1), acc)
            q = (2 + f) * cells + r
            last = series(x.at[f, 1], snaps, r) * wet[r][:, width - LANES :]
            acc = jnp.where(lane == q, pltpu.roll(last, lax.rem(q + 1, LANES), 1), acc)
        return acc

    edge[...] = lax.fori_loop(0, cells, pack, jnp.zeros((snaps, LANES), jnp.float32), unroll=UNROLL)
    for side in range(2):

        @pl.when(sends[side])
        def _():
            edge_copy(side).start()

    pass_on(0)

    def own_part(r, carry):
        l, j = r // rows, lax.rem(r, rows)
        for f in range(2):
            block = jnp.concatenate([series(x.at[f, h], snaps, r) for h in range(2)], axis=1)
            mm[f, l, j + 1] = dot(own_w, block)
        return carry

    lax.fori_loop(0, cells, own_part, 0, unroll=UNROLL)
    for c in range(1, DEPTH):
        pass_on(c)

    for side in range(2):

        @pl.when(receives[side])
        def _():
            edge_copy(side).wait_recv()

    edge_mean[...] = dot(own_w, edge[...]) + dot(
        halo_w, jnp.concatenate([edge_halo[0], edge_halo[1]], axis=0)
    )
    for side in range(2):

        @pl.when(z_sends[side])
        def _():
            mean_copy(side).start()

    wide = lax.broadcasted_iota(jnp.int32, (snaps, width), 1)

    def halo_part(r, carry):
        l, j = r // rows, lax.rem(r, rows)
        mask = wet[r]
        for f in range(2):
            block = jnp.concatenate(
                [
                    jnp.concatenate([series(halo.at[s, f, h], HALF, r) for h in range(2)], axis=1)
                    for s in range(2)
                ],
                axis=0,
            )
            mm[f, l, j + 1] = (mm[f, l, j + 1] + dot(halo_w, block)) * mask
        return carry

    def grad_x(f, r, masked, scale):
        q = (2 + f) * cells + r
        before = pltpu.roll(edge_in[0], lax.rem(2 * LANES - q, LANES), 1)
        q = f * cells + r
        after = pltpu.roll(edge_in[1], lax.rem(2 * LANES - 1 - q, LANES), 1)
        before = jnp.concatenate([before, before], axis=1)
        after = jnp.concatenate([after, after], axis=1)
        behind = jnp.where(wide == 0, before, pltpu.roll(masked, 1, 1))
        ahead = jnp.where(wide == width - 1, after, pltpu.roll(masked, width - 1, 1))
        return (ahead - behind) * scale

    def convert(l):
        def body(j, carry):
            r = l * rows + j
            mask = wet[r]
            scale_x = cx[j]
            scale_y = cy[j]
            eddy, gx, gy = [], [], []
            for f in range(2):
                masked = mm[f, l, j + 1]
                raw = jnp.concatenate([series(x.at[f, h], snaps, r) for h in range(2)], axis=1)
                eddy.append(raw - masked)
                gx.append(grad_x(f, r, masked, scale_x))
                gy.append((mm[f, l, j + 2] - mm[f, l, j]) * scale_y)
            eu, ev = eddy
            total = eu * eu * gx[0] + eu * ev * (gy[0] + gx[1]) + ev * ev * gy[1]
            conversion = -mask * total
            for h in range(2):
                cf.at[h].reshape(snaps * cells, LANES)[pl.ds(r, snaps, stride=cells), :] = conversion[
                    :, h * LANES : (h + 1) * LANES
                ]
            sums[r] = jnp.sum(conversion, axis=0, keepdims=True)
            return carry

        return body

    per_level = rows // CHUNK
    for c in range(chunks):
        finish_chunk(c)
        if c + DEPTH < chunks:
            start_chunk(c + DEPTH)
        for side in range(2):

            @pl.when(receives[side])
            def _():
                for f in range(2):
                    for h in range(2):
                        bulk(side, c, f, h).wait_recv()

        lax.fori_loop(c * CHUNK, (c + 1) * CHUNK, halo_part, 0, unroll=UNROLL)
        if c + DEPTH < chunks:
            pass_on(c + DEPTH)
        if c == 0:
            for side in range(2):

                @pl.when(z_receives[side])
                def _():
                    mean_copy(side).wait_recv()

        l, piece = c // per_level, c % per_level
        low = piece * CHUNK - (1 if piece else 0)
        high = rows if piece == per_level - 1 else (piece + 1) * CHUNK - 1
        lax.fori_loop(low, high, convert(l), 0, unroll=2)
        if piece == per_level - 1:
            part[t, l] = jnp.concatenate([sums[l * rows + j] for j in range(rows)], axis=0)
            for k in range(1, n_tm):
                part_copy(l, k, t).start()

            def narrow(s, carry):
                for h in range(2):
                    conv_ref[s, pl.ds(l * rows, rows), pl.ds(h * LANES, LANES)] = cf[
                        h, s, pl.ds(l * rows, rows), :
                    ].astype(jnp.bfloat16)
                return carry

            lax.fori_loop(0, snaps, narrow, 0)

    for l in range(levels):
        for k in range(1, n_tm):
            part_copy(l, k, lax.rem(t + n_tm - k, n_tm)).wait_recv()
        total = part[0, l]
        for s in range(1, n_tm):
            total = total + part[s, l]
        mean_ref[l] = total / (snaps * n_tm)

    for side in range(2):

        @pl.when(sends[side])
        def _():
            edge_copy(side).wait_send()

        @pl.when(z_sends[side])
        def _():
            mean_copy(side).wait_send()

        if n_tm >= 4:

            @pl.when(t == via[side])
            def _():
                for c in range(chunks):
                    for h in range(2):
                        from_relay(side, c, h).wait_send()

    for l in range(levels):
        for k in range(1, n_tm):
            part_copy(l, k, t).wait_send()


def shards(velocity_u, velocity_v, land_sea, bottom_level, spacing_x, spacing_y):
    snaps, levels, rows, width = velocity_u.shape
    cells = levels * rows
    n_tm, n_tile = lax.axis_size("tm"), lax.axis_size("tile")
    assert width == 2 * LANES and 4 * cells == LANES and snaps >= HALF and rows % CHUNK == 0
    own, halo = band_parts(snaps)
    chunks = cells // CHUNK
    vmem = pl.BlockSpec(memory_space=pltpu.VMEM)
    hbm = pl.BlockSpec(memory_space=pltpu.HBM)
    f32 = jnp.float32
    dma = pltpu.SemaphoreType.DMA
    conversion, mean_map = pl.pallas_call(
        functools.partial(kernel, n_tm, n_tile, levels),
        out_shape=(
            jax.ShapeDtypeStruct((snaps, cells, width), jnp.bfloat16),
            jax.ShapeDtypeStruct((levels, rows, width), f32),
        ),
        in_specs=[hbm] * 8,
        out_specs=(vmem, vmem),
        scratch_shapes=[
            pltpu.VMEM((rows, width), jnp.int32),
            pltpu.VMEM((rows, width), jnp.int32),
            pltpu.VMEM((rows, width), f32),
            pltpu.VMEM((rows, width), f32),
            pltpu.VMEM(own.shape, f32),
            pltpu.VMEM(halo.shape, f32),
            dma((6,)),
            pltpu.VMEM((2, 2, snaps, cells, LANES), f32),
            pltpu.VMEM((2, 2, 2, HALF, cells, LANES), f32),
            pltpu.VMEM((2, levels, rows + 2, snaps, width), f32),
            pltpu.VMEM((2, snaps, cells, LANES), f32),
            pltpu.VMEM((cells, 1, width), f32),
            pltpu.VMEM((rows, 1, width), f32),
            pltpu.VMEM((rows, 1, width), f32),
            pltpu.VMEM((cells, 1, width), f32),
            pltpu.VMEM((n_tm, levels, rows, width), f32),
            pltpu.VMEM((snaps, LANES), f32),
            pltpu.VMEM((2, HALF, LANES), f32),
            pltpu.VMEM((snaps, LANES), f32),
            pltpu.VMEM((2, snaps, LANES), f32),
            pltpu.VMEM((chunks, 2, HALF, CHUNK, LANES), f32),
            dma((chunks, 2)),
            dma((chunks, 2)),
            dma((2, 2)),
            dma((2, chunks, 2, 2)),
            dma((2, chunks, 2, 2)),
            dma((2,)),
            dma((2,)),
            dma((2,)),
            dma((2,)),
            dma((levels, n_tm)),
            dma((levels, n_tm)),
        ],
        compiler_params=pltpu.CompilerParams(
            collective_id=0, has_side_effects=True, vmem_limit_bytes=40 * 1024 * 1024
        ),
        cost_estimate=pl.CostEstimate(flops=10**9, bytes_accessed=4 * 10**6, transcendentals=0),
    )(
        velocity_u.reshape(snaps, cells, width),
        velocity_v.reshape(snaps, cells, width),
        land_sea, bottom_level, spacing_x, spacing_y,
        jnp.asarray(own), jnp.asarray(halo),
    )
    return conversion.reshape(velocity_u.shape), mean_map


def solution(mesh):
    in_specs = (
        P("tm", None, None, "tile"),
        P("tm", None, None, "tile"),
        P(None, "tile"),
        P(None, "tile"),
        P(None, "tile"),
        P(None, "tile"),
    )
    out_specs = (P("tm", None, None, "tile"), P(None, None, "tile"))
    return jax.shard_map(shards, mesh=mesh, in_specs=in_specs, out_specs=out_specs, check_vma=False)
```
